128 devices in a mesh: gx: 8 (over x, core), gy: 16 (over z, y).
Axes of the slice: x: 4, y: 4, z: 4, core: 2. Of those that a mesh axis runs over, the one named last changes fastest.
Arguments:
- normed: bfloat16 [3072, 8192], P('gy', 'gx'), may hold values from -6 to 6
- qkv_weight: bfloat16 [8192, 10240], P('gx', 'gy'), may hold values from -0.0625 to 0.0625
- out_weight: bfloat16 [8192, 8192], P('gy', 'gx'), may hold values from -0.5 to 0.5
- prompt_key_value: bfloat16 [384, 1280, 2048], P(('gx', 'gy')), may hold values from -460 to 460
- beam_key_value: bfloat16 [3072, 48, 2048], P(('gx', 'gy')), may hold values from -6 to 6
- parents: int32 [3072], P(('gx', 'gy')), may hold values from 0 to 7
- lengths: int32 [384], P(('gx', 'gy')), may hold values from 160 to 1280, as said below
Outputs:
- attn_out: bfloat16 [3072, 8192], P('gy', 'gx')
- latest_key_value: bfloat16 [3072, 2048], P(('gx', 'gy'))
The draws below stay inside these ranges and needn't reach their ends.
Inputs may be any that keep to these rules, and one draw needn't show every extreme that they name: parents numbers a beam within its prompt's 8 beams. `lengths`: some prompt has exactly 1280 cached tokens and some other exactly 160.
All inputs are finite; a program needn't handle non-finite values.
Results may differ from the reference program's by a relative error of at most 0.015.
Values may be sent and summed in bfloat16 or wider, within the bound.
No kernel may reach another device: no remote copies, remote signals or barrier semaphores. Data moves between devices by JAX's collectives and lax.ppermute only.
A program may use at most 128 MiB of HBM per device.

```python
import jax
import jax.numpy as jnp
from jax import lax

D = 8192
QUERY_HEADS = 64
KEY_HEADS = 8
HEAD_SIZE = 128
BEAMS_PER_PROMPT = 8
GENERATED_COUNT = 48
PROMPT_TOKENS = 1280
PROMPT_COUNT = 384
TOTAL_BEAMS = 3072
QKV = 10240


def draw_prompt_key_value(key, part):
    key = jax.random.fold_in(key, 11)
    random_seed_key = jax.random.fold_in(key, 0)
    prompt_cache = jax.random.truncated_normal(random_seed_key, -5.0, 5.0, (PROMPT_COUNT, PROMPT_TOKENS, 2 * KEY_HEADS * HEAD_SIZE), jnp.float32)
    return prompt_cache.astype(jnp.bfloat16)


def draw_lengths(key, part):
    key = jax.random.fold_in(key, 23)
    random_seed_key, first_key, second_key = jax.random.split(key, 3)
    counts = jax.random.randint(random_seed_key, (PROMPT_COUNT,), PROMPT_TOKENS // 8, PROMPT_TOKENS + 1)
    longest = jax.random.randint(first_key, (), 0, PROMPT_COUNT)
    shortest = (longest + 1 + jax.random.randint(second_key, (), 0, PROMPT_COUNT - 1)) % PROMPT_COUNT
    places = jnp.arange(PROMPT_COUNT, dtype=jnp.int32)
    counts = jnp.where(places == longest, PROMPT_TOKENS, counts)
    counts = jnp.where(places == shortest, PROMPT_TOKENS // 8, counts)
    return counts.astype(jnp.int32)


def plant(array, own_key, smallest, largest):
    longest = array.shape.index(max(array.shape))
    spots = []
    for shift in (0, 1):
        where = [jax.random.randint(jax.random.fold_in(own_key, axis), (), 0, length) for axis, length in enumerate(array.shape)]
        where[longest] = (where[longest] + shift) % array.shape[longest]
        spots.append(tuple(where))
    return array.at[spots[0]].set(smallest).at[spots[1]].set(largest)


def steps_of(stream_key, shape, cuts, smallest, top_value):
    level, own = 1.0, jax.random.fold_in(stream_key, 6)
    for axis_at, parts in cuts:
        steps = jnp.exp(jax.random.uniform(jax.random.fold_in(own, axis_at), (parts,), jnp.float32, smallest / len(cuts), top_value / len(cuts)))
        level = level * jnp.repeat(steps, shape[axis_at] // parts).reshape([-1 if axis == axis_at else 1 for axis in range(len(shape))])
    return level


def bell_draw(key, dims, width, limit, cuts=(), kind=jnp.bfloat16):
    entries = jax.random.normal(key, dims, jnp.float32) * width
    if len(cuts) > 0:
        entries = steps_of(key, dims, cuts, -0.22, 0.18) * entries
    return jnp.clip(entries, min=-limit, max=limit).astype(kind)


def setup_inputs(seed: int = 0) -> dict:
    splits = jax.random.split(jax.random.key(seed), 8)
    normed = bell_draw(splits[0], (TOTAL_BEAMS, D), 1.0, 6.0, ((0, 16), (1, 8)))
    qkv_weight = bell_draw(splits[1], (D, QKV), D ** -0.5, 0.0625, ((0, 8), (1, 16)))
    out_weight = bell_draw(splits[2], (QUERY_HEADS * HEAD_SIZE, D), HEAD_SIZE ** -0.5, 0.5, ((0, 16), (1, 8)))
    prompt_key_value = draw_prompt_key_value(jax.random.fold_in(splits[7], 71), 0)
    beam_key_value = bell_draw(splits[4], (TOTAL_BEAMS, GENERATED_COUNT, 2 * KEY_HEADS * HEAD_SIZE), 1.0, 6.0, ((0, 128),))
    parents = plant(jax.random.randint(splits[5], (TOTAL_BEAMS,), 0, BEAMS_PER_PROMPT), jax.random.fold_in(splits[5], 1), 0, BEAMS_PER_PROMPT - 1).astype(jnp.int32)
    lengths = draw_lengths(jax.random.fold_in(splits[7], 71), 0)
    return dict(normed=normed, qkv_weight=qkv_weight, out_weight=out_weight, prompt_key_value=prompt_key_value, beam_key_value=beam_key_value, parents=parents, lengths=lengths)


def rotary_tables(positions):
    half_dim = HEAD_SIZE // 2
    exponent = 2.0 * jnp.arange(half_dim, dtype=jnp.float32) / HEAD_SIZE
    frequency = jnp.exp(-jnp.log(jnp.float32(500000.0)) * exponent)
    angles = positions.astype(jnp.float32)[:, None] * frequency[None, :]
    return jnp.cos(angles), jnp.sin(angles)


def rotate(values, cosine, sine_table):
    half_dim = HEAD_SIZE // 2
    leading = values[..., :half_dim]
    trailing = values[..., half_dim:]
    return jnp.concatenate([leading * cosine - trailing * sine_table, trailing * cosine + leading * sine_table], axis=-1)


def to_brain(values):
    return lax.optimization_barrier(values.astype(jnp.bfloat16)).astype(jnp.float32)


def one_prompt(items):
    query_rows, beam_own_keys, beam_own_values, cached_tokens, beam_history, length = items
    grouped_queries = query_rows.reshape(BEAMS_PER_PROMPT, KEY_HEADS, QUERY_HEADS // KEY_HEADS, HEAD_SIZE).astype(jnp.float32)
    prompt_cache_keys = cached_tokens[:, : KEY_HEADS * HEAD_SIZE].reshape(PROMPT_TOKENS, KEY_HEADS, HEAD_SIZE).astype(jnp.float32)
    prompt_cache_values = cached_tokens[:, KEY_HEADS * HEAD_SIZE:].reshape(PROMPT_TOKENS, KEY_HEADS, HEAD_SIZE).astype(jnp.float32)
    earlier_keys = beam_history[:, :, : KEY_HEADS * HEAD_SIZE].reshape(BEAMS_PER_PROMPT, GENERATED_COUNT, KEY_HEADS, HEAD_SIZE).astype(jnp.float32)
    earlier_values = beam_history[:, :, KEY_HEADS * HEAD_SIZE:].reshape(BEAMS_PER_PROMPT, GENERATED_COUNT, KEY_HEADS, HEAD_SIZE).astype(jnp.float32)
    scaling = HEAD_SIZE ** -0.5
    cache_scores = jnp.einsum("bgrd,tgd->bgrt", grouped_queries, prompt_cache_keys) * scaling
    past_scores = jnp.einsum("bgrd,bsgd->bgrs", grouped_queries, earlier_keys) * scaling
    own_scores = jnp.einsum("bgrd,bgd->bgr", grouped_queries, beam_own_keys.astype(jnp.float32)) * scaling
    usable = jnp.arange(PROMPT_TOKENS, dtype=jnp.int32) < length
    highest = jnp.maximum(jnp.max(jnp.where(usable, cache_scores, -jnp.inf), axis=-1), jnp.max(past_scores, axis=-1))
    highest = jnp.maximum(highest, own_scores)
    cache_terms = jnp.where(usable, jnp.exp(cache_scores - highest[..., None]), 0.0)
    past_terms = jnp.exp(past_scores - highest[..., None])
    own_terms = jnp.exp(own_scores - highest)
    total = jnp.sum(cache_terms, axis=-1) + jnp.sum(past_terms, axis=-1) + own_terms
    cache_weights = to_brain(cache_terms / total[..., None])
    past_weights = to_brain(past_terms / total[..., None])
    own_weights = to_brain(own_terms / total)
    attended = jnp.einsum("bgrt,tgd->bgrd", cache_weights, prompt_cache_values)
    attended = attended + jnp.einsum("bgrs,bsgd->bgrd", past_weights, earlier_values)
    attended = attended + own_weights[..., None] * beam_own_values.astype(jnp.float32)[:, :, None, :]
    return attended.reshape(BEAMS_PER_PROMPT, QUERY_HEADS * HEAD_SIZE).astype(jnp.bfloat16)


def reference(normed, qkv_weight, out_weight, prompt_key_value, beam_key_value, parents, lengths):
    query_key_value = jnp.dot(normed, qkv_weight, preferred_element_type=jnp.float32).astype(jnp.bfloat16)
    query_rows = query_key_value[:, : QUERY_HEADS * HEAD_SIZE].reshape(TOTAL_BEAMS, QUERY_HEADS, HEAD_SIZE)
    latest_keys = query_key_value[:, QUERY_HEADS * HEAD_SIZE:(QUERY_HEADS + KEY_HEADS) * HEAD_SIZE].reshape(TOTAL_BEAMS, KEY_HEADS, HEAD_SIZE)
    latest_values = query_key_value[:, (QUERY_HEADS + KEY_HEADS) * HEAD_SIZE:]
    positions = jnp.repeat(lengths, BEAMS_PER_PROMPT) + GENERATED_COUNT
    cosine, sine_table = rotary_tables(positions)
    rotated_query_rows = rotate(query_rows.astype(jnp.float32), cosine[:, None, :], sine_table[:, None, :]).astype(jnp.bfloat16)
    rotated_key_rows = rotate(latest_keys.astype(jnp.float32), cosine[:, None, :], sine_table[:, None, :]).astype(jnp.bfloat16)
    latest_key_value = jnp.concatenate([rotated_key_rows.reshape(TOTAL_BEAMS, KEY_HEADS * HEAD_SIZE), latest_values], axis=1)
    source = (jnp.arange(TOTAL_BEAMS, dtype=jnp.int32) // BEAMS_PER_PROMPT) * BEAMS_PER_PROMPT + parents.astype(jnp.int32)
    beam_histories = jnp.take(beam_key_value, source, axis=0)
    attended = lax.map(one_prompt, (
        rotated_query_rows.reshape(PROMPT_COUNT, BEAMS_PER_PROMPT, QUERY_HEADS, HEAD_SIZE),
        rotated_key_rows.reshape(PROMPT_COUNT, BEAMS_PER_PROMPT, KEY_HEADS, HEAD_SIZE),
        latest_values.reshape(PROMPT_COUNT, BEAMS_PER_PROMPT, KEY_HEADS, HEAD_SIZE),
        prompt_key_value,
        beam_histories.reshape(PROMPT_COUNT, BEAMS_PER_PROMPT, GENERATED_COUNT, 2 * KEY_HEADS * HEAD_SIZE),
        lengths,
    ))
    attended = attended.reshape(TOTAL_BEAMS, QUERY_HEADS * HEAD_SIZE)
    attn_out = jnp.dot(attended, out_weight, preferred_element_type=jnp.float32).astype(jnp.bfloat16)
    return (attn_out, latest_key_value)
```

```python
import functools

import jax
import jax.numpy as jnp
from jax import lax
from jax.experimental import pallas as pl
from jax.experimental.pallas import tpu as pltpu
from jax.sharding import Mesh
from jax.sharding import PartitionSpec as P

QUERY_HEADS = 64
KEY_HEADS = 8
HEAD_SIZE = 128
BEAMS_PER_PROMPT = 8
MASKED = -1e30


def rotary_tables(positions):
    half_dim = HEAD_SIZE // 2
    exponent = 2.0 * jnp.arange(half_dim, dtype=jnp.float32) / HEAD_SIZE
    frequency = jnp.exp(-jnp.log(jnp.float32(500000.0)) * exponent)
    angles = positions.astype(jnp.float32)[:, None] * frequency[None, :]
    cosine, sine = jnp.cos(angles), jnp.sin(angles)
    return (
        jnp.concatenate([cosine, cosine], axis=1)[:, None, :],
        jnp.concatenate([-sine, sine], axis=1)[:, None, :],
    )


def attend_kernel(
    prompt, parents_ref, lengths_ref, terms_ref, cos_ref, sin_ref, pkv_ref, bkv_ref, out_ref, fresh_ref
):
    beams, size = BEAMS_PER_PROMPT, HEAD_SIZE
    ratio = QUERY_HEADS // KEY_HEADS
    rows = beams * ratio
    context = pkv_ref.shape[1]
    past = bkv_ref.shape[0]
    generated = past // beams
    length = lengths_ref[prompt]
    cosine = jnp.broadcast_to(cos_ref[0], (beams, size))
    sine = jnp.broadcast_to(sin_ref[0], (beams, size))
    scale = size ** (-0.5) * 1.4426950408889634
    held = terms_ref.shape[-1] // size
    given = out_ref.shape[-1] // size

    def head(h):
        at = slice((h % held) * size, (h % held + 1) * size)
        total = terms_ref[0, h // held, :, at].astype(jnp.float32)
        for i in range(1, terms_ref.shape[0]):
            total = total + terms_ref[i, h // held, :, at].astype(jnp.float32)
        return total.astype(jnp.bfloat16).astype(jnp.float32)

    def rotated(v):
        v = v * cosine + pltpu.roll(v, size // 2, 1) * sine
        return v.astype(jnp.bfloat16).astype(jnp.float32)

    usable = lax.broadcasted_iota(jnp.int32, (rows, context), 1) < length
    beam = lax.rem(lax.broadcasted_iota(jnp.int32, (rows, past), 0), beams)
    first = jnp.zeros((rows, past), jnp.int32)
    for b in range(beams):
        first = jnp.where(beam == b, parents_ref[prompt * beams + b] * generated, first)
    place = lax.broadcasted_iota(jnp.int32, (rows, past), 1)
    chosen = (place >= first) & (place < first + generated)
    across = (((1,), (1,)), ((), ()))
    along = (((1,), (0,)), ((), ()))
    for g in range(KEY_HEADS):
        ks = slice(g * size, (g + 1) * size)
        vs = slice((KEY_HEADS + g) * size, (KEY_HEADS + g + 1) * size)
        q = jnp.concatenate([rotated(head(g * ratio + r)) for r in range(ratio)], axis=0)
        own_key = rotated(head(QUERY_HEADS + g))
        own_value = head(QUERY_HEADS + KEY_HEADS + g)
        fresh_ref[:, ks] = own_key.astype(jnp.bfloat16)
        fresh_ref[:, vs] = own_value.astype(jnp.bfloat16)
        qb = q.astype(jnp.bfloat16)
        s1 = lax.dot_general(qb, pkv_ref[0, :, ks], across, preferred_element_type=jnp.float32)
        s2 = lax.dot_general(qb, bkv_ref[:, ks], across, preferred_element_type=jnp.float32)
        s3 = jnp.sum(q * jnp.concatenate([own_key] * ratio, axis=0), axis=1, keepdims=True)
        s1 = jnp.where(usable, s1, MASKED)
        s2 = jnp.where(chosen, s2, MASKED)
        top = jnp.maximum(jnp.max(s1, axis=1, keepdims=True), jnp.max(s2, axis=1, keepdims=True))
        top = jnp.maximum(top, s3)
        e1 = jnp.exp2((s1 - top) * scale)
        e2 = jnp.exp2((s2 - top) * scale)
        e3 = jnp.exp2((s3 - top) * scale)
        total = jnp.sum(e1, axis=1, keepdims=True) + jnp.sum(e2, axis=1, keepdims=True) + e3
        o = lax.dot_general(
            e1.astype(jnp.bfloat16), pkv_ref[0, :, vs], along, preferred_element_type=jnp.float32
        )
        o = o + lax.dot_general(
            e2.astype(jnp.bfloat16), bkv_ref[:, vs], along, preferred_element_type=jnp.float32
        )
        o = (o + e3 * jnp.concatenate([own_value] * ratio, axis=0)) / total
        for r in range(ratio):
            h = g * ratio + r
            at = slice((h % given) * size, (h % given + 1) * size)
            out_ref[h // given, :, at] = o[r * beams : (r + 1) * beams].astype(jnp.bfloat16)


def attend(prompt, terms, cosine, sine, pkv, bkv, parents, lengths):
    prompts, context, width = pkv.shape
    past = bkv.shape[0] // prompts
    slabs = terms.shape[1]
    given = QUERY_HEADS * HEAD_SIZE // slabs
    grid_spec = pltpu.PrefetchScalarGridSpec(
        num_scalar_prefetch=2,
        grid=(1,),
        in_specs=[
            pl.BlockSpec(terms.shape, lambda i, *_: (0, 0, 0, 0)),
            pl.BlockSpec((1, 1, HEAD_SIZE), lambda i, *_: (prompt, 0, 0)),
            pl.BlockSpec((1, 1, HEAD_SIZE), lambda i, *_: (prompt, 0, 0)),
            pl.BlockSpec((1, context, width), lambda i, *_: (prompt, 0, 0)),
            pl.BlockSpec((past, width), lambda i, *_: (prompt, 0)),
        ],
        out_specs=[
            pl.BlockSpec((slabs, BEAMS_PER_PROMPT, given), lambda i, *_: (0, 0, 0)),
            pl.BlockSpec((BEAMS_PER_PROMPT, width), lambda i, *_: (0, 0)),
        ],
    )
    return pl.pallas_call(
        functools.partial(attend_kernel, prompt),
        grid_spec=grid_spec,
        out_shape=[
            jax.ShapeDtypeStruct((slabs, BEAMS_PER_PROMPT, given), jnp.bfloat16),
            jax.ShapeDtypeStruct((BEAMS_PER_PROMPT, width), jnp.bfloat16),
        ],
        compiler_params=pltpu.CompilerParams(vmem_limit_bytes=32 * 1024 * 1024),
        cost_estimate=pl.CostEstimate(
            flops=4 * 64 * HEAD_SIZE * KEY_HEADS * (context + past),
            bytes_accessed=2 * width * (context + past),
            transcendentals=64 * KEY_HEADS * (context + past),
        ),
    )(parents, lengths, terms, cosine, sine, pkv, bkv)


SWAP = [(0, 1), (1, 0)]


def body(normed, qkv_weight, out_weight, prompt_key_value, beam_key_value, parents, lengths):
    prompts = prompt_key_value.shape[0]
    beams = BEAMS_PER_PROMPT
    nx, nz, ny = lax.axis_size("x"), lax.axis_size("z"), lax.axis_size("y")
    core = lax.axis_index("core")
    slabs = nz * ny
    depth, columns = qkv_weight.shape
    width = out_weight.shape[0]
    plane = ("x", "z", "y")
    cosine, sine = rotary_tables(lengths + beam_key_value.shape[1])
    history = beam_key_value.reshape(-1, beam_key_value.shape[-1])
    parts = normed.reshape(-1, prompts, beams, depth)
    results, fresh = [], []
    for c in range(prompts):
        rows = lax.all_gather(parts[:, c].reshape(-1, depth), ("z", "y"), axis=0, tiled=True)
        terms = jnp.dot(rows, qkv_weight, preferred_element_type=jnp.float32)
        terms = terms.reshape(nx, 2, slabs, beams, columns)
        away = lax.dynamic_index_in_dim(terms, 1 - core, 1, keepdims=False).astype(jnp.bfloat16)
        mine = lax.dynamic_index_in_dim(terms, core, 1, keepdims=False)
        mine = (mine + lax.ppermute(away, "core", SWAP).astype(jnp.float32)).astype(jnp.bfloat16)
        mine = mine.reshape(nx * slabs, beams, columns)
        arrived = lax.all_to_all(mine, plane, split_axis=0, concat_axis=0, tiled=True)
        arrived = arrived.reshape(nx, slabs, beams, columns)
        out, new = attend(
            c, arrived, cosine, sine, prompt_key_value, history, parents, lengths
        )
        fresh.append(new)
        copies = jnp.broadcast_to(out[None], (nx,) + out.shape).reshape(nx * slabs, beams, width)
        spread = lax.all_to_all(copies, plane, split_axis=0, concat_axis=0, tiled=True)
        spread = spread.reshape(nx, slabs * beams, width)
        twin = lax.ppermute(spread, "core", SWAP)
        both = jnp.stack(
            [jnp.where(core == 0, spread, twin), jnp.where(core == 0, twin, spread)], axis=1
        )
        product = jnp.dot(
            both.reshape(-1, width), out_weight, preferred_element_type=jnp.float32
        ).astype(jnp.bfloat16)
        result = lax.psum_scatter(product, ("z", "y"), scatter_dimension=0, tiled=True)
        results.append(result.reshape(-1, beams, out_weight.shape[1]))
    result = jnp.stack(results, axis=1).reshape(-1, out_weight.shape[1])
    return (result, jnp.concatenate(fresh, axis=0))


def solution(mesh):
    chips = Mesh(mesh.devices.reshape(4, 2, 4, 4), ("x", "core", "z", "y"))
    gx, gy = ("x", "core"), ("z", "y")
    whole = gx + gy
    return jax.shard_map(
        body,
        mesh=chips,
        in_specs=(
            P(gy, gx),
            P(gx, gy),
            P(gy, gx),
            P(whole, None, None),
            P(whole, None, None),
            P(whole),
            P(whole),
        ),
        out_specs=(P(gy, gx), P(whole, None)),
        check_vma=False,
    )
```

```python
import functools

import jax
import jax.numpy as jnp
from jax import lax
from jax.experimental import pallas as pl
from jax.experimental.pallas import tpu as pltpu
from jax.sharding import Mesh
from jax.sharding import PartitionSpec as P

QUERY_HEADS = 64
KEY_HEADS = 8
HEAD_SIZE = 128
BEAMS_PER_PROMPT = 8
MASKED = -1e30


def rotary_tables(positions):
    half_dim = HEAD_SIZE // 2
    exponent = 2.0 * jnp.arange(half_dim, dtype=jnp.float32) / HEAD_SIZE
    frequency = jnp.exp(-jnp.log(jnp.float32(500000.0)) * exponent)
    angles = positions.astype(jnp.float32)[:, None] * frequency[None, :]
    cosine, sine = jnp.cos(angles), jnp.sin(angles)
    return (
        jnp.concatenate([cosine, cosine], axis=1)[:, None, :],
        jnp.concatenate([-sine, sine], axis=1)[:, None, :],
    )


def attend_kernel(
    parents_ref, lengths_ref, sources_ref, terms_ref, cos_ref, sin_ref, pkv_ref, bkv_ref,
    out_ref, fresh_ref, slab_ref,
):
    prompt = pl.program_id(0)
    beams, size = BEAMS_PER_PROMPT, HEAD_SIZE
    ratio = QUERY_HEADS // KEY_HEADS
    rows = beams * ratio
    context = pkv_ref.shape[1]
    past = bkv_ref.shape[0]
    generated = past // beams
    length = lengths_ref[prompt]
    cosine = jnp.broadcast_to(cos_ref[0], (beams, size))
    sine = jnp.broadcast_to(sin_ref[0], (beams, size))
    scale = size ** (-0.5) * 1.4426950408889634
    given = out_ref.shape[-1] // size
    slabs, _, columns = slab_ref.shape
    held = columns // size
    for n in range(slabs):
        slab_ref[n] = terms_ref[sources_ref[n], 0].astype(jnp.float32)

    def head(h):
        return slab_ref[h // held, :, (h % held) * size : (h % held + 1) * size]

    def rotated(v):
        v = v * cosine + pltpu.roll(v, size // 2, 1) * sine
        return v.astype(jnp.bfloat16).astype(jnp.float32)

    usable = lax.broadcasted_iota(jnp.int32, (2 * rows, context), 1) < length
    beam = lax.rem(lax.broadcasted_iota(jnp.int32, (2 * rows, past), 0), beams)
    first = jnp.zeros((2 * rows, past), jnp.int32)
    for b in range(beams):
        first = jnp.where(beam == b, parents_ref[prompt * beams + b] * generated, first)
    place = lax.broadcasted_iota(jnp.int32, (2 * rows, past), 1)
    chosen = (place >= first) & (place < first + generated)
    across = (((1,), (1,)), ((), ()))
    along = (((1,), (0,)), ((), ()))
    for j in range(KEY_HEADS // 2):
        ks = slice(2 * j * size, 2 * (j + 1) * size)
        vs = slice((KEY_HEADS + 2 * j) * size, (KEY_HEADS + 2 * j + 2) * size)
        queries, own_values, own_scores = [], [], []
        for g in (2 * j, 2 * j + 1):
            q = jnp.concatenate([rotated(head(g * ratio + r)) for r in range(ratio)], axis=0)
            own_key = rotated(head(QUERY_HEADS + g))
            own_value = head(QUERY_HEADS + KEY_HEADS + g)
            fresh_ref[0, :, g * size : (g + 1) * size] = own_key.astype(jnp.bfloat16)
            fresh_ref[0, :, (KEY_HEADS + g) * size : (KEY_HEADS + g + 1) * size] = own_value.astype(
                jnp.bfloat16
            )
            own_scores.append(
                jnp.sum(q * jnp.concatenate([own_key] * ratio, axis=0), axis=1, keepdims=True)
            )
            queries.append(q)
            own_values.append(jnp.concatenate([own_value] * ratio, axis=0))
        zero = jnp.zeros((rows, size), jnp.float32)
        q = jnp.concatenate(
            [
                jnp.concatenate([queries[0], zero], axis=1),
                jnp.concatenate([zero, queries[1]], axis=1),
            ],
            axis=0,
        ).astype(jnp.bfloat16)
        s1 = lax.dot_general(q, pkv_ref[0, :, ks], across, preferred_element_type=jnp.float32)
        s2 = lax.dot_general(q, bkv_ref[:, ks], across, preferred_element_type=jnp.float32)
        s3 = jnp.concatenate(own_scores, axis=0)
        s1 = jnp.where(usable, s1, MASKED)
        s2 = jnp.where(chosen, s2, MASKED)
        top = jnp.maximum(jnp.max(s1, axis=1, keepdims=True), jnp.max(s2, axis=1, keepdims=True))
        top = jnp.maximum(top, s3)
        e1 = jnp.exp2((s1 - top) * scale)
        e2 = jnp.exp2((s2 - top) * scale)
        e3 = jnp.exp2((s3 - top) * scale)
        total = jnp.sum(e1, axis=1, keepdims=True) + jnp.sum(e2, axis=1, keepdims=True) + e3
        o = lax.dot_general(
            e1.astype(jnp.bfloat16), pkv_ref[0, :, vs], along, preferred_element_type=jnp.float32
        )
        o = o + lax.dot_general(
            e2.astype(jnp.bfloat16), bkv_ref[:, vs], along, preferred_element_type=jnp.float32
        )
        for i in range(2):
            at = slice(i * rows, (i + 1) * rows)
            part = o[at, i * size : (i + 1) * size]
            part = (part + e3[at] * own_values[i]) / total[at]
            for r in range(ratio):
                h = (2 * j + i) * ratio + r
                lanes = slice((h % given) * size, (h % given + 1) * size)
                out_ref[h // given, 0, :, lanes] = part[r * beams : (r + 1) * beams].astype(
                    jnp.bfloat16
                )


def attend(terms, sources, cosine, sine, pkv, bkv, parents, lengths, groups):
    prompts, context, width = pkv.shape
    past = bkv.shape[0] // prompts
    count, _, beams, columns = terms.shape
    slabs = sources.shape[0]
    given = QUERY_HEADS * HEAD_SIZE // groups
    grid_spec = pltpu.PrefetchScalarGridSpec(
        num_scalar_prefetch=3,
        grid=(prompts,),
        in_specs=[
            pl.BlockSpec((count, 1, beams, columns), lambda i, *_: (0, i, 0, 0)),
            pl.BlockSpec((1, 1, HEAD_SIZE), lambda i, *_: (i, 0, 0)),
            pl.BlockSpec((1, 1, HEAD_SIZE), lambda i, *_: (i, 0, 0)),
            pl.BlockSpec((1, context, width), lambda i, *_: (i, 0, 0)),
            pl.BlockSpec((past, width), lambda i, *_: (i, 0)),
        ],
        out_specs=[
            pl.BlockSpec((groups, 1, beams, given), lambda i, *_: (0, i, 0, 0)),
            pl.BlockSpec((1, beams, width), lambda i, *_: (i, 0, 0)),
        ],
        scratch_shapes=[pltpu.VMEM((slabs, beams, columns), jnp.float32)],
    )
    return pl.pallas_call(
        attend_kernel,
        grid_spec=grid_spec,
        out_shape=[
            jax.ShapeDtypeStruct((groups, prompts, beams, given), jnp.bfloat16),
            jax.ShapeDtypeStruct((prompts, beams, width), jnp.bfloat16),
        ],
        compiler_params=pltpu.CompilerParams(vmem_limit_bytes=56 * 1024 * 1024),
        cost_estimate=pl.CostEstimate(
            flops=4 * prompts * 64 * HEAD_SIZE * KEY_HEADS * (context + past),
            bytes_accessed=2 * prompts * width * (context + past),
            transcendentals=prompts * 64 * KEY_HEADS * (context + past),
        ),
    )(parents, lengths, sources, terms, cosine, sine, pkv, bkv)


def project_kernel(which_ref, places_ref, *refs):
    *row_refs, own_ref, other_ref, out_ref, row_buffer, weight_buffer, row_sems, weight_sem = refs
    count, rows, depth = row_buffer.shape
    for which, ref in enumerate((own_ref, other_ref)):

        @pl.when(which_ref[0] == which)
        def _(ref=ref):
            pltpu.make_async_copy(ref, weight_buffer, weight_sem).start()

    copies, at = [], 0
    for s, ref in enumerate(row_refs):
        piece = row_buffer.at[at // rows, pl.ds(at % rows, ref.shape[0])]
        copies.append(pltpu.make_async_copy(ref, piece, row_sems.at[s]))
        copies[-1].start()
        at += ref.shape[0]
    pltpu.make_async_copy(own_ref, weight_buffer, weight_sem).wait()
    for copy in copies:
        copy.wait()
    product = jnp.dot(
        row_buffer[...].reshape(count * rows, depth),
        weight_buffer[...],
        preferred_element_type=jnp.float32,
    ).astype(jnp.bfloat16)
    for s in range(count):
        out_ref[places_ref[s]] = product[s * rows : (s + 1) * rows]


def project(which, places, gathered, own, other):
    rows, depth = gathered[0].shape
    count = sum(part.shape[0] for part in gathered) // rows
    columns = own.shape[1]
    scalars = pl.BlockSpec(memory_space=pltpu.SMEM)
    return pl.pallas_call(
        project_kernel,
        in_specs=[scalars, scalars]
        + [pl.BlockSpec(memory_space=pl.ANY)] * (len(gathered) + 2),
        out_specs=pl.BlockSpec(memory_space=pltpu.VMEM),
        out_shape=jax.ShapeDtypeStruct((count, rows, columns), jnp.bfloat16),
        scratch_shapes=[
            pltpu.VMEM((count, rows, depth), jnp.bfloat16),
            pltpu.VMEM((depth, columns), jnp.bfloat16),
            pltpu.SemaphoreType.DMA((len(gathered),)),
            pltpu.SemaphoreType.DMA,
        ],
        compiler_params=pltpu.CompilerParams(vmem_limit_bytes=56 * 1024 * 1024),
        cost_estimate=pl.CostEstimate(
            flops=2 * count * rows * depth * columns,
            bytes_accessed=2 * (count * rows * (depth + columns) + depth * columns),
            transcendentals=0,
        ),
    )(which.reshape(1), places, *gathered, own, other)


def output_kernel(core_ref, rows_ref, weight_ref, *refs):
    out_ref = refs[-1]
    xs, _, rows, _ = out_ref.shape
    product = jnp.dot(
        rows_ref[...], weight_ref[...], preferred_element_type=jnp.float32
    ).astype(jnp.bfloat16)
    for x in range(xs):
        out_ref[x, 0] = product[x * rows : (x + 1) * rows]


def output(core, value, weight, xs, buffer=None):
    rows, depth = value.shape
    columns = weight.shape[1]
    step = 256
    shape = (xs, 2, rows // xs, columns)
    grid_spec = pltpu.PrefetchScalarGridSpec(
        num_scalar_prefetch=1,
        grid=(columns // step,),
        in_specs=[
            pl.BlockSpec((rows, depth), lambda n, core: (0, 0)),
            pl.BlockSpec((depth, step), lambda n, core: (0, n)),
        ]
        + ([] if buffer is None else [pl.BlockSpec(memory_space=pl.ANY)]),
        out_specs=pl.BlockSpec((xs, 1, rows // xs, step), lambda n, core: (0, core[0], 0, n)),
    )
    return pl.pallas_call(
        output_kernel,
        grid_spec=grid_spec,
        out_shape=jax.ShapeDtypeStruct(shape, jnp.bfloat16),
        input_output_aliases={} if buffer is None else {3: 0},
        compiler_params=pltpu.CompilerParams(vmem_limit_bytes=32 * 1024 * 1024),
        cost_estimate=pl.CostEstimate(
            flops=2 * rows * depth * columns,
            bytes_accessed=2 * (rows * (depth + columns) + depth * columns),
            transcendentals=0,
        ),
    )(core.reshape(1), value, weight, *([] if buffer is None else [buffer]))


SWAP = [(0, 1), (1, 0)]


def shifted(value, axis, shift):
    size = lax.axis_size(axis)
    return lax.ppermute(value, axis, [(i, (i + shift) % size) for i in range(size)])


def beside(value, axis):
    return [value, shifted(value, axis, 1), shifted(value, axis, 3)]


def relayed(blocks, axis):
    value, near, back = blocks
    half = value.shape[0] // 2
    return [value, near, shifted(near[:half], axis, 1), shifted(back[half:], axis, 3), back]


def body(normed, qkv_weight, out_weight, prompt_key_value, beam_key_value, parents, lengths):
    prompts = prompt_key_value.shape[0]
    beams = BEAMS_PER_PROMPT
    nx, nz, ny = lax.axis_size("x"), lax.axis_size("z"), lax.axis_size("y")
    core = lax.axis_index("core")
    z, y = lax.axis_index("z"), lax.axis_index("y")
    depth, columns = qkv_weight.shape
    mine_rows = prompts * beams

    other = lax.ppermute(qkv_weight, "y", [(i, ny - 1 - i) for i in range(ny)])
    own = beside(normed, "z")
    swapped = lax.ppermute(normed, "y", [(i, i ^ 1) for i in range(ny)])
    *own, swapped = lax.optimization_barrier((*own, swapped))
    swapped = beside(swapped, "z")
    own = relayed(own, "z")
    swapped = relayed(swapped, "z")
    out_weight, other = lax.optimization_barrier((out_weight, other))
    weight = lax.all_gather(out_weight, "y", axis=0, tiled=True)

    cosine, sine = rotary_tables(lengths + beam_key_value.shape[1])
    history = beam_key_value.reshape(-1, beam_key_value.shape[-1])
    slab = jnp.arange(nz * ny, dtype=jnp.int32)
    slab_z, slab_y = slab // ny, slab % ny
    slots = jnp.where(slab_y // 2 == core, 0, 1)
    sender_y = jnp.where(slots == 0, slab_y, ny - 1 - slab_y)
    sources = (jnp.where(slots == core, 0, nz) + slab_z) * 2 + sender_y % 2
    sources = sources.astype(jnp.int32)
    from_z = (z - jnp.arange(nz, dtype=jnp.int32)) % nz
    places = jnp.concatenate([from_z * 2 + y % 2, from_z * 2 + 1 - y % 2]).astype(jnp.int32)
    core = core.astype(jnp.int32)

    gathered = own + swapped
    away = project(1 - core, places, gathered, qkv_weight, other)
    arrived = lax.ppermute(away, "core", SWAP)
    mine = project(core, places, gathered, qkv_weight, other)
    terms = (mine.astype(jnp.float32) + arrived.astype(jnp.float32)).astype(jnp.bfloat16)
    terms = terms.reshape(nx * nz * ny, mine_rows, columns)
    terms = lax.all_to_all(terms, ("x", "z", "y"), split_axis=0, concat_axis=0, tiled=True)
    terms = jnp.sum(terms.reshape(nx, nz, 2, 2, mine_rows, columns).astype(jnp.float32), axis=0)
    terms = terms.astype(jnp.bfloat16)
    kept = lax.dynamic_index_in_dim(terms, core, 1, keepdims=False)
    passed = lax.dynamic_index_in_dim(terms, 1 - core, 1, keepdims=False)
    terms = jnp.stack([kept, lax.ppermute(passed, "core", SWAP)])
    terms = terms.reshape(4 * nz, prompts, beams, columns)
    out, fresh = attend(
        terms, sources, cosine, sine, prompt_key_value, history, parents, lengths, nz
    )
    out = out.reshape(nz, mine_rows, -1)
    copies = jnp.broadcast_to(out[None], (nx,) + out.shape).reshape((nx * nz,) + out.shape[1:])
    mine = lax.all_to_all(copies, ("x", "z"), split_axis=0, concat_axis=0, tiled=True)
    mine = mine.reshape(nx * nz * mine_rows, -1)
    twin = lax.ppermute(mine, "core", SWAP)
    product = output(core, mine, weight, nx)
    product = output(1 - core, twin, weight, nx, product)
    product = product.reshape(nz * ny, 2 * mine_rows, -1)
    terms = lax.all_to_all(product, ("z", "y"), split_axis=0, concat_axis=0, tiled=True)
    terms = terms.reshape(nz, ny, 2, mine_rows, -1).astype(jnp.float32)
    result = jnp.sum(terms, axis=0).astype(jnp.bfloat16).transpose(1, 0, 2, 3)
    return (result.reshape(-1, result.shape[-1]), fresh.reshape(mine_rows, -1))


def solution(mesh):
    chips = Mesh(mesh.devices.reshape(4, 2, 4, 4), ("x", "core", "z", "y"))
    gx, gy = ("x", "core"), ("z", "y")
    whole = gx + gy
    return jax.shard_map(
        body,
        mesh=chips,
        in_specs=(
            P(gy, gx),
            P(gx, gy),
            P(gy, gx),
            P(whole, None, None),
            P(whole, None, None),
            P(whole),
            P(whole),
        ),
        out_specs=(P(gy, gx), P(whole, None)),
        check_vma=False,
    )
```

```python
import functools

import jax
import jax.numpy as jnp
from jax import lax
from jax.experimental import pallas as pl
from jax.experimental.pallas import tpu as pltpu
from jax.sharding import Mesh
from jax.sharding import PartitionSpec as P

QUERY_HEADS = 64
KEY_HEADS = 8
HEAD_SIZE = 128
BEAMS_PER_PROMPT = 8
MASKED = -1e30


def rotary_tables(positions):
    half_dim = HEAD_SIZE // 2
    exponent = 2.0 * jnp.arange(half_dim, dtype=jnp.float32) / HEAD_SIZE
    frequency = jnp.exp(-jnp.log(jnp.float32(500000.0)) * exponent)
    angles = positions.astype(jnp.float32)[:, None] * frequency[None, :]
    cosine, sine = jnp.cos(angles), jnp.sin(angles)
    return (
        jnp.concatenate([cosine, cosine], axis=1)[:, None, :],
        jnp.concatenate([-sine, sine], axis=1)[:, None, :],
    )


def attend_kernel(
    parents_ref, lengths_ref, sources_ref, terms_ref, cos_ref, sin_ref, pkv_ref, bkv_ref,
    out_ref, fresh_ref, slab_ref,
):
    prompt = pl.program_id(0)
    beams, size = BEAMS_PER_PROMPT, HEAD_SIZE
    ratio = QUERY_HEADS // KEY_HEADS
    rows = beams * ratio
    context = pkv_ref.shape[1]
    past = bkv_ref.shape[0]
    generated = past // beams
    length = lengths_ref[prompt]
    cosine = jnp.broadcast_to(cos_ref[0], (beams, size))
    sine = jnp.broadcast_to(sin_ref[0], (beams, size))
    scale = size ** (-0.5) * 1.4426950408889634
    given = out_ref.shape[-1] // size
    slabs, _, columns = slab_ref.shape
    held = columns // size
    for n in range(slabs):
        slab_ref[n] = terms_ref[sources_ref[n], 0].astype(jnp.float32)

    def head(h):
        return slab_ref[h // held, :, (h % held) * size : (h % held + 1) * size]

    def rotated(v):
        v = v * cosine + pltpu.roll(v, size // 2, 1) * sine
        return v.astype(jnp.bfloat16).astype(jnp.float32)

    usable = lax.broadcasted_iota(jnp.int32, (2 * rows, context), 1) < length
    beam = lax.rem(lax.broadcasted_iota(jnp.int32, (2 * rows, past), 0), beams)
    first = jnp.zeros((2 * rows, past), jnp.int32)
    for b in range(beams):
        first = jnp.where(beam == b, parents_ref[prompt * beams + b] * generated, first)
    place = lax.broadcasted_iota(jnp.int32, (2 * rows, past), 1)
    chosen = (place >= first) & (place < first + generated)
    across = (((1,), (1,)), ((), ()))
    along = (((1,), (0,)), ((), ()))
    for j in range(KEY_HEADS // 2):
        ks = slice(2 * j * size, 2 * (j + 1) * size)
        vs = slice((KEY_HEADS + 2 * j) * size, (KEY_HEADS + 2 * j + 2) * size)
        queries, own_values, own_scores = [], [], []
        for g in (2 * j, 2 * j + 1):
            q = jnp.concatenate([rotated(head(g * ratio + r)) for r in range(ratio)], axis=0)
            own_key = rotated(head(QUERY_HEADS + g))
            own_value = head(QUERY_HEADS + KEY_HEADS + g)
            fresh_ref[0, :, g * size : (g + 1) * size] = own_key.astype(jnp.bfloat16)
            fresh_ref[0, :, (KEY_HEADS + g) * size : (KEY_HEADS + g + 1) * size] = own_value.astype(
                jnp.bfloat16
            )
            own_scores.append(
                jnp.sum(q * jnp.concatenate([own_key] * ratio, axis=0), axis=1, keepdims=True)
            )
            queries.append(q)
            own_values.append(jnp.concatenate([own_value] * ratio, axis=0))
        zero = jnp.zeros((rows, size), jnp.float32)
        q = jnp.concatenate(
            [
                jnp.concatenate([queries[0], zero], axis=1),
                jnp.concatenate([zero, queries[1]], axis=1),
            ],
            axis=0,
        ).astype(jnp.bfloat16)
        s1 = lax.dot_general(q, pkv_ref[0, :, ks], across, preferred_element_type=jnp.float32)
        s2 = lax.dot_general(q, bkv_ref[:, ks], across, preferred_element_type=jnp.float32)
        s3 = jnp.concatenate(own_scores, axis=0)
        s1 = jnp.where(usable, s1, MASKED)
        s2 = jnp.where(chosen, s2, MASKED)
        top = jnp.maximum(jnp.max(s1, axis=1, keepdims=True), jnp.max(s2, axis=1, keepdims=True))
        top = jnp.maximum(top, s3)
        e1 = jnp.exp2((s1 - top) * scale)
        e2 = jnp.exp2((s2 - top) * scale)
        e3 = jnp.exp2((s3 - top) * scale)
        total = jnp.sum(e1, axis=1, keepdims=True) + jnp.sum(e2, axis=1, keepdims=True) + e3
        o = lax.dot_general(
            e1.astype(jnp.bfloat16), pkv_ref[0, :, vs], along, preferred_element_type=jnp.float32
        )
        o = o + lax.dot_general(
            e2.astype(jnp.bfloat16), bkv_ref[:, vs], along, preferred_element_type=jnp.float32
        )
        for i in range(2):
            at = slice(i * rows, (i + 1) * rows)
            part = o[at, i * size : (i + 1) * size]
            part = ((part + e3[at] * own_values[i]) / total[at]).astype(jnp.bfloat16)
            for r in range(ratio):
                h = (2 * j + i) * ratio + r
                lanes = slice((h % given) * size, (h % given + 1) * size)
                for c in range(out_ref.shape[0]):
                    out_ref[c, h // given, 0, :, lanes] = part[r * beams : (r + 1) * beams]


def attend(terms, sources, cosine, sine, pkv, bkv, parents, lengths, groups, copies):
    prompts, context, width = pkv.shape
    past = bkv.shape[0] // prompts
    count, _, beams, columns = terms.shape
    slabs = sources.shape[0]
    given = QUERY_HEADS * HEAD_SIZE // groups
    grid_spec = pltpu.PrefetchScalarGridSpec(
        num_scalar_prefetch=3,
        grid=(prompts,),
        in_specs=[
            pl.BlockSpec((count, 1, beams, columns), lambda i, *_: (0, i, 0, 0)),
            pl.BlockSpec((1, 1, HEAD_SIZE), lambda i, *_: (i, 0, 0)),
            pl.BlockSpec((1, 1, HEAD_SIZE), lambda i, *_: (i, 0, 0)),
            pl.BlockSpec((1, context, width), lambda i, *_: (i, 0, 0)),
            pl.BlockSpec((past, width), lambda i, *_: (i, 0)),
        ],
        out_specs=[
            pl.BlockSpec((copies, groups, 1, beams, given), lambda i, *_: (0, 0, i, 0, 0)),
            pl.BlockSpec((1, beams, width), lambda i, *_: (i, 0, 0)),
        ],
        scratch_shapes=[pltpu.VMEM((slabs, beams, columns), jnp.float32)],
    )
    return pl.pallas_call(
        attend_kernel,
        grid_spec=grid_spec,
        out_shape=[
            jax.ShapeDtypeStruct((copies, groups, prompts, beams, given), jnp.bfloat16),
            jax.ShapeDtypeStruct((prompts, beams, width), jnp.bfloat16),
        ],
        compiler_params=pltpu.CompilerParams(vmem_limit_bytes=56 * 1024 * 1024),
        cost_estimate=pl.CostEstimate(
            flops=4 * prompts * 64 * HEAD_SIZE * KEY_HEADS * (context + past),
            bytes_accessed=2 * prompts * width * (context + past),
            transcendentals=prompts * 64 * KEY_HEADS * (context + past),
        ),
    )(parents, lengths, sources, terms, cosine, sine, pkv, bkv)


def project_kernel(core_ref, places_ref, *refs):
    *row_refs, own_ref, other_ref, mine_ref, away_ref = refs[:-7]
    row_buffer, weight_buffer, mine_buffer, away_buffer, row_sems, weight_sems, out_sems = refs[-7:]
    count, rows, depth = row_buffer.shape
    half = count // 2

    def fetch(i):
        for core, pair in enumerate(((own_ref, other_ref), (other_ref, own_ref))):

            @pl.when(core_ref[0] == core)
            def _(pair=pair):
                pltpu.make_async_copy(pair[i], weight_buffer.at[i], weight_sems.at[i]).start()

    arriving, at = [[], []], 0
    for s, ref in enumerate(row_refs):
        if s == 0:
            fetch(1)
        elif s == len(row_refs) // 2:
            fetch(0)
        piece = row_buffer.at[at // rows, pl.ds(at % rows, ref.shape[0])]
        copy = pltpu.make_async_copy(ref, piece, row_sems.at[s])
        copy.start()
        arriving[at // (half * rows)].append(copy)
        at += ref.shape[0]
    leaving = []
    for i, buffer, out_ref in ((1, away_buffer, away_ref), (0, mine_buffer, mine_ref)):
        pltpu.make_async_copy(own_ref, weight_buffer.at[i], weight_sems.at[i]).wait()
        for h in range(2):
            if i == 1:
                for copy in arriving[h]:
                    copy.wait()
            product = jnp.dot(
                row_buffer[h * half : (h + 1) * half].reshape(half * rows, depth),
                weight_buffer[i],
                preferred_element_type=jnp.float32,
            ).astype(jnp.bfloat16)
            for s in range(half):
                k = h * half + s
                buffer[k] = product[s * rows : (s + 1) * rows]
                copy = pltpu.make_async_copy(
                    buffer.at[k], out_ref.at[places_ref[k]], out_sems.at[i * count + k]
                )
                copy.start()
                leaving.append(copy)
    for copy in leaving:
        copy.wait()


def project(core, places, gathered, own, other):
    rows, depth = gathered[0].shape
    count = sum(part.shape[0] for part in gathered) // rows
    columns = own.shape[1]
    scalars = pl.BlockSpec(memory_space=pltpu.SMEM)
    far = pl.BlockSpec(memory_space=pl.ANY)
    return pl.pallas_call(
        project_kernel,
        in_specs=[scalars, scalars] + [far] * (len(gathered) + 2),
        out_specs=[far, far],
        out_shape=[jax.ShapeDtypeStruct((count, rows, columns), jnp.bfloat16)] * 2,
        scratch_shapes=[
            pltpu.VMEM((count, rows, depth), jnp.bfloat16),
            pltpu.VMEM((2, depth, columns), jnp.bfloat16),
            pltpu.VMEM((count, rows, columns), jnp.bfloat16),
            pltpu.VMEM((count, rows, columns), jnp.bfloat16),
            pltpu.SemaphoreType.DMA((len(gathered),)),
            pltpu.SemaphoreType.DMA((2,)),
            pltpu.SemaphoreType.DMA((2 * count,)),
        ],
        compiler_params=pltpu.CompilerParams(vmem_limit_bytes=56 * 1024 * 1024),
        cost_estimate=pl.CostEstimate(
            flops=4 * count * rows * depth * columns,
            bytes_accessed=2 * (count * rows * (depth + 2 * columns) + 2 * depth * columns),
            transcendentals=0,
        ),
    )(core.reshape(1), places, *gathered, own, other)


def add_kernel(a_ref, b_ref, out_ref):
    total = a_ref[...].astype(jnp.float32) + b_ref[...].astype(jnp.float32)
    out_ref[...] = total.astype(jnp.bfloat16)


def add(a, b):
    count, rows, columns = a.shape
    block = pl.BlockSpec((2, rows, columns), lambda i: (i, 0, 0))
    return pl.pallas_call(
        add_kernel,
        grid=(count // 2,),
        in_specs=[block, block],
        out_specs=block,
        out_shape=jax.ShapeDtypeStruct(a.shape, jnp.bfloat16),
        compiler_params=pltpu.CompilerParams(vmem_limit_bytes=24 * 1024 * 1024),
        cost_estimate=pl.CostEstimate(
            flops=count * rows * columns, bytes_accessed=6 * count * rows * columns, transcendentals=0
        ),
    )(a, b)


def output_kernel(core_ref, rows_ref, weight_ref, *refs):
    out_ref = refs[-1]
    xs, _, rows, _ = out_ref.shape
    product = jnp.dot(
        rows_ref[...], weight_ref[...], preferred_element_type=jnp.float32
    ).astype(jnp.bfloat16)
    for x in range(xs):
        out_ref[x, 0] = product[x * rows : (x + 1) * rows]


def output(core, value, weight, xs, buffer=None):
    rows, depth = value.shape
    columns = weight.shape[1]
    step = 256
    shape = (xs, 2, rows // xs, columns)
    grid_spec = pltpu.PrefetchScalarGridSpec(
        num_scalar_prefetch=1,
        grid=(columns // step,),
        in_specs=[
            pl.BlockSpec((rows, depth), lambda n, core: (0, 0)),
            pl.BlockSpec((depth, step), lambda n, core: (0, n)),
        ]
        + ([] if buffer is None else [pl.BlockSpec(memory_space=pl.ANY)]),
        out_specs=pl.BlockSpec((xs, 1, rows // xs, step), lambda n, core: (0, core[0], 0, n)),
    )
    return pl.pallas_call(
        output_kernel,
        grid_spec=grid_spec,
        out_shape=jax.ShapeDtypeStruct(shape, jnp.bfloat16),
        input_output_aliases={} if buffer is None else {3: 0},
        compiler_params=pltpu.CompilerParams(vmem_limit_bytes=32 * 1024 * 1024),
        cost_estimate=pl.CostEstimate(
            flops=2 * rows * depth * columns,
            bytes_accessed=2 * (rows * (depth + columns) + depth * columns),
            transcendentals=0,
        ),
    )(core.reshape(1), value, weight, *([] if buffer is None else [buffer]))


SWAP = [(0, 1), (1, 0)]


def shifted(value, axis, shift):
    size = lax.axis_size(axis)
    return lax.ppermute(value, axis, [(i, (i + shift) % size) for i in range(size)])


def beside(value, axis):
    return [value, shifted(value, axis, 1), shifted(value, axis, 3)]


def relayed(blocks, axis):
    value, near, back = blocks
    half = value.shape[0] // 2
    return [value, near, shifted(near[:half], axis, 1), shifted(back[half:], axis, 3), back]


def body(normed, qkv_weight, out_weight, prompt_key_value, beam_key_value, parents, lengths):
    prompts = prompt_key_value.shape[0]
    beams = BEAMS_PER_PROMPT
    nx, nz, ny = lax.axis_size("x"), lax.axis_size("z"), lax.axis_size("y")
    core = lax.axis_index("core")
    z, y = lax.axis_index("z"), lax.axis_index("y")
    depth, columns = qkv_weight.shape
    mine_rows = prompts * beams

    other = lax.ppermute(qkv_weight, "y", [(i, ny - 1 - i) for i in range(ny)])
    own = beside(normed, "z")
    swapped = lax.ppermute(normed, "y", [(i, i ^ 1) for i in range(ny)])
    *own, swapped = lax.optimization_barrier((*own, swapped))
    swapped = beside(swapped, "z")
    own = relayed(own, "z")
    swapped = relayed(swapped, "z")
    out_weight, other = lax.optimization_barrier((out_weight, other))
    weight = lax.all_gather(out_weight, "y", axis=0, tiled=True)

    cosine, sine = rotary_tables(lengths + beam_key_value.shape[1])
    history = beam_key_value.reshape(-1, beam_key_value.shape[-1])
    slab = jnp.arange(nz * ny, dtype=jnp.int32)
    slab_z, slab_y = slab // ny, slab % ny
    slots = jnp.where(slab_y // 2 == core, 0, 1)
    sender_y = jnp.where(slots == 0, slab_y, ny - 1 - slab_y)
    sources = (jnp.where(slots == core, 0, nz) + slab_z) * 2 + sender_y % 2
    sources = sources.astype(jnp.int32)
    from_z = (z - jnp.arange(nz, dtype=jnp.int32)) % nz
    places = jnp.concatenate([from_z * 2 + y % 2, from_z * 2 + 1 - y % 2]).astype(jnp.int32)
    core = core.astype(jnp.int32)

    mine, away = project(core, places, own + swapped, qkv_weight, other)
    terms = add(mine, lax.ppermute(away, "core", SWAP))
    terms = terms.reshape(nx * nz * ny, mine_rows, columns)
    terms = lax.all_to_all(terms, ("x", "z", "y"), split_axis=0, concat_axis=0, tiled=True)
    terms = jnp.sum(terms.reshape(nx, nz, 2, 2, mine_rows, columns).astype(jnp.float32), axis=0)
    terms = terms.astype(jnp.bfloat16)
    kept = lax.dynamic_index_in_dim(terms, core, 1, keepdims=False)
    passed = lax.dynamic_index_in_dim(terms, 1 - core, 1, keepdims=False)
    terms = jnp.stack([kept, lax.ppermute(passed, "core", SWAP)])
    terms = terms.reshape(4 * nz, prompts, beams, columns)
    out, fresh = attend(
        terms, sources, cosine, sine, prompt_key_value, history, parents, lengths, nz, nx
    )
    copies = out.reshape(nx * nz, mine_rows, -1)
    mine = lax.all_to_all(copies, ("x", "z"), split_axis=0, concat_axis=0, tiled=True)
    mine = mine.reshape(nx * nz * mine_rows, -1)
    twin = lax.ppermute(mine, "core", SWAP)
    product = output(core, mine, weight, nx)
    product = output(1 - core, twin, weight, nx, product)
    product = product.reshape(nz * ny, 2 * mine_rows, -1)
    terms = lax.all_to_all(product, ("z", "y"), split_axis=0, concat_axis=0, tiled=True)
    terms = terms.reshape(nz, ny, 2, mine_rows, -1).astype(jnp.float32)
    result = jnp.sum(terms, axis=0).astype(jnp.bfloat16).transpose(1, 0, 2, 3)
    return (result.reshape(-1, result.shape[-1]), fresh.reshape(mine_rows, -1))


def solution(mesh):
    chips = Mesh(mesh.devices.reshape(4, 2, 4, 4), ("x", "core", "z", "y"))
    gx, gy = ("x", "core"), ("z", "y")
    whole = gx + gy
    return jax.shard_map(
        body,
        mesh=chips,
        in_specs=(
            P(gy, gx),
            P(gx, gy),
            P(gy, gx),
            P(whole, None, None),
            P(whole, None, None),
            P(whole),
            P(whole),
        ),
        out_specs=(P(gy, gx), P(whole, None)),
        check_vma=False,
    )
```

```python
import functools

import jax
import jax.numpy as jnp
from jax import lax
from jax.experimental import pallas as pl
from jax.experimental.pallas import tpu as pltpu
from jax.sharding import Mesh
from jax.sharding import PartitionSpec as P

QUERY_HEADS = 64
KEY_HEADS = 8
HEAD_SIZE = 128
BEAMS_PER_PROMPT = 8
MASKED = -1e30


def rotary_tables(positions):
    half_dim = HEAD_SIZE // 2
    exponent = 2.0 * jnp.arange(half_dim, dtype=jnp.float32) / HEAD_SIZE
    frequency = jnp.exp(-jnp.log(jnp.float32(500000.0)) * exponent)
    angles = positions.astype(jnp.float32)[:, None] * frequency[None, :]
    cosine, sine = jnp.cos(angles), jnp.sin(angles)
    rows = [
        jnp.concatenate([cosine, cosine], axis=1),
        jnp.concatenate([-sine, sine], axis=1),
    ]
    return jnp.concatenate(rows, axis=0)[:, None, :]


def attend_kernel(
    parents_ref, lengths_ref, sources_ref, terms_ref, cos_ref, sin_ref, pkv_ref, bkv_ref,
    out_ref, fresh_ref, slab_ref,
):
    prompt = pl.program_id(0)
    beams, size = BEAMS_PER_PROMPT, HEAD_SIZE
    ratio = QUERY_HEADS // KEY_HEADS
    rows = beams * ratio
    context = pkv_ref.shape[1]
    past = bkv_ref.shape[0]
    generated = past // beams
    length = lengths_ref[prompt]
    cosine = jnp.broadcast_to(cos_ref[0], (beams, size))
    sine = jnp.broadcast_to(sin_ref[0], (beams, size))
    scale = size ** (-0.5) * 1.4426950408889634
    given = out_ref.shape[-1] // size
    slabs, _, columns = slab_ref.shape
    held = columns // size
    for n in range(slabs):
        slab_ref[n] = terms_ref[sources_ref[n], 0].astype(jnp.float32)

    def head(h):
        return slab_ref[h // held, :, (h % held) * size : (h % held + 1) * size]

    def rotated(v):
        v = v * cosine + pltpu.roll(v, size // 2, 1) * sine
        return v.astype(jnp.bfloat16).astype(jnp.float32)

    usable = lax.broadcasted_iota(jnp.int32, (2 * rows, context), 1) < length
    beam = lax.rem(lax.broadcasted_iota(jnp.int32, (2 * rows, past), 0), beams)
    first = jnp.zeros((2 * rows, past), jnp.int32)
    for b in range(beams):
        first = jnp.where(beam == b, parents_ref[prompt * beams + b] * generated, first)
    place = lax.broadcasted_iota(jnp.int32, (2 * rows, past), 1)
    chosen = (place >= first) & (place < first + generated)
    across = (((1,), (1,)), ((), ()))
    along = (((1,), (0,)), ((), ()))
    for j in range(KEY_HEADS // 2):
        ks = slice(2 * j * size, 2 * (j + 1) * size)
        vs = slice((KEY_HEADS + 2 * j) * size, (KEY_HEADS + 2 * j + 2) * size)
        queries, own_values, own_scores = [], [], []
        for g in (2 * j, 2 * j + 1):
            q = jnp.concatenate([rotated(head(g * ratio + r)) for r in range(ratio)], axis=0)
            own_key = rotated(head(QUERY_HEADS + g))
            own_value = head(QUERY_HEADS + KEY_HEADS + g)
            fresh_ref[0, :, g * size : (g + 1) * size] = own_key.astype(jnp.bfloat16)
            fresh_ref[0, :, (KEY_HEADS + g) * size : (KEY_HEADS + g + 1) * size] = own_value.astype(
                jnp.bfloat16
            )
            own_scores.append(
                jnp.sum(q * jnp.concatenate([own_key] * ratio, axis=0), axis=1, keepdims=True)
            )
            queries.append(q)
            own_values.append(jnp.concatenate([own_value] * ratio, axis=0))
        zero = jnp.zeros((rows, size), jnp.float32)
        q = jnp.concatenate(
            [
                jnp.concatenate([queries[0], zero], axis=1),
                jnp.concatenate([zero, queries[1]], axis=1),
            ],
            axis=0,
        ).astype(jnp.bfloat16)
        s1 = lax.dot_general(q, pkv_ref[0, :, ks], across, preferred_element_type=jnp.float32)
        s2 = lax.dot_general(q, bkv_ref[:, ks], across, preferred_element_type=jnp.float32)
        s3 = jnp.concatenate(own_scores, axis=0)
        s1 = jnp.where(usable, s1, MASKED)
        s2 = jnp.where(chosen, s2, MASKED)
        top = jnp.maximum(jnp.max(s1, axis=1, keepdims=True), jnp.max(s2, axis=1, keepdims=True))
        top = jnp.maximum(top, s3)
        e1 = jnp.exp2((s1 - top) * scale)
        e2 = jnp.exp2((s2 - top) * scale)
        e3 = jnp.exp2((s3 - top) * scale)
        total = jnp.sum(e1, axis=1, keepdims=True) + jnp.sum(e2, axis=1, keepdims=True) + e3
        o = lax.dot_general(
            e1.astype(jnp.bfloat16), pkv_ref[0, :, vs], along, preferred_element_type=jnp.float32
        )
        o = o + lax.dot_general(
            e2.astype(jnp.bfloat16), bkv_ref[:, vs], along, preferred_element_type=jnp.float32
        )
        for i in range(2):
            at = slice(i * rows, (i + 1) * rows)
            part = o[at, i * size : (i + 1) * size]
            part = ((part + e3[at] * own_values[i]) / total[at]).astype(jnp.bfloat16)
            for r in range(ratio):
                h = (2 * j + i) * ratio + r
                lanes = slice((h % given) * size, (h % given + 1) * size)
                for c in range(out_ref.shape[0]):
                    out_ref[c, h // given, 0, :, lanes] = part[r * beams : (r + 1) * beams]


def attend(terms, sources, tables, pkv, bkv, parents, lengths, groups, copies):
    prompts, context, width = pkv.shape
    past = bkv.shape[0] // prompts
    count, _, beams, columns = terms.shape
    slabs = sources.shape[0]
    given = QUERY_HEADS * HEAD_SIZE // groups
    grid_spec = pltpu.PrefetchScalarGridSpec(
        num_scalar_prefetch=3,
        grid=(prompts,),
        in_specs=[
            pl.BlockSpec((count, 1, beams, columns), lambda i, *_: (0, i, 0, 0)),
            pl.BlockSpec((1, 1, HEAD_SIZE), lambda i, *_: (i, 0, 0)),
            pl.BlockSpec((1, 1, HEAD_SIZE), lambda i, *_: (prompts + i, 0, 0)),
            pl.BlockSpec((1, context, width), lambda i, *_: (i, 0, 0)),
            pl.BlockSpec((past, width), lambda i, *_: (i, 0)),
        ],
        out_specs=[
            pl.BlockSpec((copies, groups, 1, beams, given), lambda i, *_: (0, 0, i, 0, 0)),
            pl.BlockSpec((1, beams, width), lambda i, *_: (i, 0, 0)),
        ],
        scratch_shapes=[pltpu.VMEM((slabs, beams, columns), jnp.float32)],
    )
    return pl.pallas_call(
        attend_kernel,
        grid_spec=grid_spec,
        out_shape=[
            jax.ShapeDtypeStruct((copies, groups, prompts, beams, given), jnp.bfloat16),
            jax.ShapeDtypeStruct((prompts, beams, width), jnp.bfloat16),
        ],
        compiler_params=pltpu.CompilerParams(vmem_limit_bytes=56 * 1024 * 1024),
        cost_estimate=pl.CostEstimate(
            flops=4 * prompts * 64 * HEAD_SIZE * KEY_HEADS * (context + past),
            bytes_accessed=2 * prompts * width * (context + past),
            transcendentals=prompts * 64 * KEY_HEADS * (context + past),
        ),
    )(parents, lengths, sources, terms, tables, tables, pkv, bkv)


def project_kernel(core_ref, places_ref, *refs):
    *row_refs, own_ref, other_ref, mine_ref, away_ref = refs[:-7]
    row_buffer, weight_buffer, mine_buffer, away_buffer, row_sems, weight_sems, out_sems = refs[-7:]
    count, rows, depth = row_buffer.shape
    half = count // 2

    def fetch(i):
        for core, pair in enumerate(((own_ref, other_ref), (other_ref, own_ref))):

            @pl.when(core_ref[0] == core)
            def _(pair=pair):
                pltpu.make_async_copy(pair[i], weight_buffer.at[i], weight_sems.at[i]).start()

    arriving, at = [[], []], 0
    for s, ref in enumerate(row_refs):
        if s == 0:
            fetch(1)
        elif s == len(row_refs) // 2:
            fetch(0)
        piece = row_buffer.at[at // rows, pl.ds(at % rows, ref.shape[0])]
        copy = pltpu.make_async_copy(ref, piece, row_sems.at[s])
        copy.start()
        arriving[at // (half * rows)].append(copy)
        at += ref.shape[0]
    leaving = []
    for i, buffer, out_ref in ((1, away_buffer, away_ref), (0, mine_buffer, mine_ref)):
        pltpu.make_async_copy(own_ref, weight_buffer.at[i], weight_sems.at[i]).wait()
        for h in range(2):
            if i == 1:
                for copy in arriving[h]:
                    copy.wait()
            product = jnp.dot(
                row_buffer[h * half : (h + 1) * half].reshape(half * rows, depth),
                weight_buffer[i],
                preferred_element_type=jnp.float32,
            ).astype(jnp.bfloat16)
            for s in range(half):
                k = h * half + s
                buffer[k] = product[s * rows : (s + 1) * rows]
                copy = pltpu.make_async_copy(
                    buffer.at[k], out_ref.at[places_ref[k]], out_sems.at[i * count + k]
                )
                copy.start()
                leaving.append(copy)
    for copy in leaving:
        copy.wait()


def project(core, places, gathered, own, other):
    rows, depth = gathered[0].shape
    count = sum(part.shape[0] for part in gathered) // rows
    columns = own.shape[1]
    scalars = pl.BlockSpec(memory_space=pltpu.SMEM)
    far = pl.BlockSpec(memory_space=pl.ANY)
    return pl.pallas_call(
        project_kernel,
        in_specs=[scalars, scalars] + [far] * (len(gathered) + 2),
        out_specs=[far, far],
        out_shape=[jax.ShapeDtypeStruct((count, rows, columns), jnp.bfloat16)] * 2,
        scratch_shapes=[
            pltpu.VMEM((count, rows, depth), jnp.bfloat16),
            pltpu.VMEM((2, depth, columns), jnp.bfloat16),
            pltpu.VMEM((count, rows, columns), jnp.bfloat16),
            pltpu.VMEM((count, rows, columns), jnp.bfloat16),
            pltpu.SemaphoreType.DMA((len(gathered),)),
            pltpu.SemaphoreType.DMA((2,)),
            pltpu.SemaphoreType.DMA((2 * count,)),
        ],
        compiler_params=pltpu.CompilerParams(vmem_limit_bytes=56 * 1024 * 1024),
        cost_estimate=pl.CostEstimate(
            flops=4 * count * rows * depth * columns,
            bytes_accessed=2 * (count * rows * (depth + 2 * columns) + 2 * depth * columns),
            transcendentals=0,
        ),
    )(core.reshape(1), places, *gathered, own, other)


def add_kernel(a_ref, b_ref, out_ref):
    total = a_ref[...].astype(jnp.float32) + b_ref[...].astype(jnp.float32)
    out_ref[...] = total.astype(jnp.bfloat16)


def add(a, b):
    count, rows, columns = a.shape
    block = pl.BlockSpec((2, rows, columns), lambda i: (i, 0, 0))
    return pl.pallas_call(
        add_kernel,
        grid=(count // 2,),
        in_specs=[block, block],
        out_specs=block,
        out_shape=jax.ShapeDtypeStruct(a.shape, jnp.bfloat16),
        compiler_params=pltpu.CompilerParams(vmem_limit_bytes=24 * 1024 * 1024),
        cost_estimate=pl.CostEstimate(
            flops=count * rows * columns, bytes_accessed=6 * count * rows * columns, transcendentals=0
        ),
    )(a, b)


def output_kernel(core_ref, rows_ref, weight_ref, *refs):
    out_ref = refs[-1]
    xs, _, rows, _ = out_ref.shape
    product = jnp.dot(
        rows_ref[...], weight_ref[...], preferred_element_type=jnp.float32
    ).astype(jnp.bfloat16)
    for x in range(xs):
        out_ref[x, 0] = product[x * rows : (x + 1) * rows]


def output(core, value, weight, xs, buffer=None):
    rows, depth = value.shape
    columns = weight.shape[1]
    step = 256
    shape = (xs, 2, rows // xs, columns)
    grid_spec = pltpu.PrefetchScalarGridSpec(
        num_scalar_prefetch=1,
        grid=(columns // step,),
        in_specs=[
            pl.BlockSpec((rows, depth), lambda n, core: (0, 0)),
            pl.BlockSpec((depth, step), lambda n, core: (0, n)),
        ]
        + ([] if buffer is None else [pl.BlockSpec(memory_space=pl.ANY)]),
        out_specs=pl.BlockSpec((xs, 1, rows // xs, step), lambda n, core: (0, core[0], 0, n)),
    )
    return pl.pallas_call(
        output_kernel,
        grid_spec=grid_spec,
        out_shape=jax.ShapeDtypeStruct(shape, jnp.bfloat16),
        input_output_aliases={} if buffer is None else {3: 0},
        compiler_params=pltpu.CompilerParams(vmem_limit_bytes=32 * 1024 * 1024),
        cost_estimate=pl.CostEstimate(
            flops=2 * rows * depth * columns,
            bytes_accessed=2 * (rows * (depth + columns) + depth * columns),
            transcendentals=0,
        ),
    )(core.reshape(1), value, weight, *([] if buffer is None else [buffer]))


SWAP = [(0, 1), (1, 0)]


def shifted(value, axis, shift):
    size = lax.axis_size(axis)
    return lax.ppermute(value, axis, [(i, (i + shift) % size) for i in range(size)])


def beside(value, axis):
    return [value, shifted(value, axis, 1), shifted(value, axis, 3)]


def relayed(blocks, axis):
    value, near, back = blocks
    half = value.shape[0] // 2
    return [value, near, shifted(near[:half], axis, 1), shifted(back[half:], axis, 3), back]


def body(normed, qkv_weight, out_weight, prompt_key_value, beam_key_value, parents, lengths):
    prompts = prompt_key_value.shape[0]
    beams = BEAMS_PER_PROMPT
    nx, nz, ny = lax.axis_size("x"), lax.axis_size("z"), lax.axis_size("y")
    core = lax.axis_index("core")
    z, y = lax.axis_index("z"), lax.axis_index("y")
    depth, columns = qkv_weight.shape
    mine_rows = prompts * beams

    other = lax.ppermute(qkv_weight, "y", [(i, ny - 1 - i) for i in range(ny)])
    own = beside(normed, "z")
    swapped = lax.ppermute(normed, "y", [(i, i ^ 1) for i in range(ny)])
    tables = rotary_tables(lengths + beam_key_value.shape[1])
    slab = jnp.arange(nz * ny, dtype=jnp.int32)
    slab_z, slab_y = slab // ny, slab % ny
    slots = jnp.where(slab_y // 2 == core, 0, 1)
    sender_y = jnp.where(slots == 0, slab_y, ny - 1 - slab_y)
    sources = (jnp.where(slots == core, 0, nz) + slab_z) * 2 + sender_y % 2
    sources = sources.astype(jnp.int32)
    from_z = (z - jnp.arange(nz, dtype=jnp.int32)) % nz
    places = jnp.concatenate([from_z * 2 + y % 2, from_z * 2 + 1 - y % 2]).astype(jnp.int32)
    core = core.astype(jnp.int32)
    small = (tables, sources, places)
    (*own, swapped), small = lax.optimization_barrier(((*own, swapped), small))
    tables, sources, places = small
    swapped = beside(swapped, "z")
    own = relayed(own, "z")
    swapped = relayed(swapped, "z")
    out_weight, other = lax.optimization_barrier((out_weight, other))
    weight = lax.all_gather(out_weight, "y", axis=0, tiled=True)

    history = beam_key_value.reshape(-1, beam_key_value.shape[-1])
    mine, away = project(core, places, own + swapped, qkv_weight, other)
    terms = add(mine, lax.ppermute(away, "core", SWAP))
    terms = terms.reshape(nx * nz * ny, mine_rows, columns)
    terms = lax.all_to_all(terms, ("x", "z", "y"), split_axis=0, concat_axis=0, tiled=True)
    terms = jnp.sum(terms.reshape(nx, nz, 2, 2, mine_rows, columns).astype(jnp.float32), axis=0)
    terms = terms.astype(jnp.bfloat16)
    kept = lax.dynamic_index_in_dim(terms, core, 1, keepdims=False)
    passed = lax.dynamic_index_in_dim(terms, 1 - core, 1, keepdims=False)
    terms = jnp.stack([kept, lax.ppermute(passed, "core", SWAP)])
    terms = terms.reshape(4 * nz, prompts, beams, columns)
    out, fresh = attend(
        terms, sources, tables, prompt_key_value, history, parents, lengths, nz, nx
    )
    copies = out.reshape(nx * nz, mine_rows, -1)
    mine = lax.all_to_all(copies, ("x", "z"), split_axis=0, concat_axis=0, tiled=True)
    mine = mine.reshape(nx * nz * mine_rows, -1)
    twin = lax.ppermute(mine, "core", SWAP)
    product = output(core, mine, weight, nx)
    product = output(1 - core, twin, weight, nx, product)
    product = product.reshape(nz * ny, 2 * mine_rows, -1)
    terms = lax.all_to_all(product, ("z", "y"), split_axis=0, concat_axis=0, tiled=True)
    terms = terms.reshape(nz, ny, 2, mine_rows, -1).astype(jnp.float32)
    result = jnp.sum(terms, axis=0).astype(jnp.bfloat16).transpose(1, 0, 2, 3)
    return (result.reshape(-1, result.shape[-1]), fresh.reshape(mine_rows, -1))


def solution(mesh):
    chips = Mesh(mesh.devices.reshape(4, 2, 4, 4), ("x", "core", "z", "y"))
    gx, gy = ("x", "core"), ("z", "y")
    whole = gx + gy
    return jax.shard_map(
        body,
        mesh=chips,
        in_specs=(
            P(gy, gx),
            P(gx, gy),
            P(gy, gx),
            P(whole, None, None),
            P(whole, None, None),
            P(whole),
            P(whole),
        ),
        out_specs=(P(gy, gx), P(whole, None)),
        check_vma=False,
    )
```

```python
import functools

import jax
import jax.numpy as jnp
from jax import lax
from jax.experimental import pallas as pl
from jax.experimental.pallas import tpu as pltpu
from jax.sharding import Mesh
from jax.sharding import PartitionSpec as P

QUERY_HEADS = 64
KEY_HEADS = 8
HEAD_SIZE = 128
BEAMS_PER_PROMPT = 8
MASKED = -1e30


def rotary_tables(positions):
    half_dim = HEAD_SIZE // 2
    exponent = 2.0 * jnp.arange(half_dim, dtype=jnp.float32) / HEAD_SIZE
    frequency = jnp.exp(-jnp.log(jnp.float32(500000.0)) * exponent)
    angles = positions.astype(jnp.float32)[:, None] * frequency[None, :]
    cosine, sine = jnp.cos(angles), jnp.sin(angles)
    rows = [
        jnp.concatenate([cosine, cosine], axis=1),
        jnp.concatenate([-sine, sine], axis=1),
    ]
    return jnp.concatenate(rows, axis=0)[:, None, :]


def attend_kernel(
    parents_ref, lengths_ref, sources_ref, terms_ref, cos_ref, sin_ref, pkv_ref, bkv_ref,
    out_ref, fresh_ref, slab_ref,
):
    prompt = pl.program_id(0)
    beams, size = BEAMS_PER_PROMPT, HEAD_SIZE
    ratio = QUERY_HEADS // KEY_HEADS
    rows = beams * ratio
    context = pkv_ref.shape[1]
    past = bkv_ref.shape[0]
    generated = past // beams
    length = lengths_ref[prompt]
    cosine = jnp.broadcast_to(cos_ref[0], (beams, size))
    sine = jnp.broadcast_to(sin_ref[0], (beams, size))
    scale = size ** (-0.5) * 1.4426950408889634
    given = out_ref.shape[-1] // size
    slabs, _, columns = slab_ref.shape
    held = columns // size
    for n in range(slabs):
        slab_ref[n] = terms_ref[sources_ref[n], 0].astype(jnp.float32)

    def head(h):
        return slab_ref[h // held, :, (h % held) * size : (h % held + 1) * size]

    def rotated(v):
        v = v * cosine + pltpu.roll(v, size // 2, 1) * sine
        return v.astype(jnp.bfloat16).astype(jnp.float32)

    usable = lax.broadcasted_iota(jnp.int32, (2 * rows, context), 1) < length
    beam = lax.rem(lax.broadcasted_iota(jnp.int32, (2 * rows, past), 0), beams)
    first = jnp.zeros((2 * rows, past), jnp.int32)
    for b in range(beams):
        first = jnp.where(beam == b, parents_ref[prompt * beams + b] * generated, first)
    place = lax.broadcasted_iota(jnp.int32, (2 * rows, past), 1)
    chosen = (place >= first) & (place < first + generated)
    across = (((1,), (1,)), ((), ()))
    along = (((1,), (0,)), ((), ()))
    for j in range(KEY_HEADS // 2):
        ks = slice(2 * j * size, 2 * (j + 1) * size)
        vs = slice((KEY_HEADS + 2 * j) * size, (KEY_HEADS + 2 * j + 2) * size)
        queries, own_values, own_scores = [], [], []
        for g in (2 * j, 2 * j + 1):
            q = jnp.concatenate([rotated(head(g * ratio + r)) for r in range(ratio)], axis=0)
            own_key = rotated(head(QUERY_HEADS + g))
            own_value = head(QUERY_HEADS + KEY_HEADS + g)
            fresh_ref[0, :, g * size : (g + 1) * size] = own_key.astype(jnp.bfloat16)
            fresh_ref[0, :, (KEY_HEADS + g) * size : (KEY_HEADS + g + 1) * size] = own_value.astype(
                jnp.bfloat16
            )
            own_scores.append(
                jnp.sum(q * jnp.concatenate([own_key] * ratio, axis=0), axis=1, keepdims=True)
            )
            queries.append(q)
            own_values.append(jnp.concatenate([own_value] * ratio, axis=0))
        zero = jnp.zeros((rows, size), jnp.float32)
        q = jnp.concatenate(
            [
                jnp.concatenate([queries[0], zero], axis=1),
                jnp.concatenate([zero, queries[1]], axis=1),
            ],
            axis=0,
        ).astype(jnp.bfloat16)
        s1 = lax.dot_general(q, pkv_ref[0, :, ks], across, preferred_element_type=jnp.float32)
        s2 = lax.dot_general(q, bkv_ref[:, ks], across, preferred_element_type=jnp.float32)
        s3 = jnp.concatenate(own_scores, axis=0)
        s1 = jnp.where(usable, s1, MASKED)
        s2 = jnp.where(chosen, s2, MASKED)
        top = jnp.maximum(jnp.max(s1, axis=1, keepdims=True), jnp.max(s2, axis=1, keepdims=True))
        top = jnp.maximum(top, s3)
        e1 = jnp.exp2((s1 - top) * scale)
        e2 = jnp.exp2((s2 - top) * scale)
        e3 = jnp.exp2((s3 - top) * scale)
        total = jnp.sum(e1, axis=1, keepdims=True) + jnp.sum(e2, axis=1, keepdims=True) + e3
        o = lax.dot_general(
            e1.astype(jnp.bfloat16), pkv_ref[0, :, vs], along, preferred_element_type=jnp.float32
        )
        o = o + lax.dot_general(
            e2.astype(jnp.bfloat16), bkv_ref[:, vs], along, preferred_element_type=jnp.float32
        )
        for i in range(2):
            at = slice(i * rows, (i + 1) * rows)
            part = o[at, i * size : (i + 1) * size]
            part = ((part + e3[at] * own_values[i]) / total[at]).astype(jnp.bfloat16)
            for r in range(ratio):
                h = (2 * j + i) * ratio + r
                lanes = slice((h % given) * size, (h % given + 1) * size)
                for c in range(out_ref.shape[0]):
                    out_ref[c, h // given, 0, :, lanes] = part[r * beams : (r + 1) * beams]


def attend(terms, sources, tables, pkv, bkv, parents, lengths, groups, copies):
    prompts, context, width = pkv.shape
    past = bkv.shape[0] // prompts
    count, _, beams, columns = terms.shape
    slabs = sources.shape[0]
    given = QUERY_HEADS * HEAD_SIZE // groups
    grid_spec = pltpu.PrefetchScalarGridSpec(
        num_scalar_prefetch=3,
        grid=(prompts,),
        in_specs=[
            pl.BlockSpec((count, 1, beams, columns), lambda i, *_: (0, i, 0, 0)),
            pl.BlockSpec((1, 1, HEAD_SIZE), lambda i, *_: (i, 0, 0)),
            pl.BlockSpec((1, 1, HEAD_SIZE), lambda i, *_: (prompts + i, 0, 0)),
            pl.BlockSpec((1, context, width), lambda i, *_: (i, 0, 0)),
            pl.BlockSpec((past, width), lambda i, *_: (i, 0)),
        ],
        out_specs=[
            pl.BlockSpec((copies, groups, 1, beams, given), lambda i, *_: (0, 0, i, 0, 0)),
            pl.BlockSpec((1, beams, width), lambda i, *_: (i, 0, 0)),
        ],
        scratch_shapes=[pltpu.VMEM((slabs, beams, columns), jnp.float32)],
    )
    return pl.pallas_call(
        attend_kernel,
        grid_spec=grid_spec,
        out_shape=[
            jax.ShapeDtypeStruct((copies, groups, prompts, beams, given), jnp.bfloat16),
            jax.ShapeDtypeStruct((prompts, beams, width), jnp.bfloat16),
        ],
        compiler_params=pltpu.CompilerParams(vmem_limit_bytes=50 * 1024 * 1024),
        cost_estimate=pl.CostEstimate(
            flops=4 * prompts * 64 * HEAD_SIZE * KEY_HEADS * (context + past),
            bytes_accessed=2 * prompts * width * (context + past),
            transcendentals=prompts * 64 * KEY_HEADS * (context + past),
        ),
    )(parents, lengths, sources, terms, tables, tables, pkv, bkv)


def project_kernel(core_ref, places_ref, *refs):
    *row_refs, own_ref, other_ref, mine_ref, away_ref = refs[:-7]
    row_buffer, weight_buffer, mine_buffer, away_buffer, row_sems, weight_sems, out_sems = refs[-7:]
    count, rows, depth = row_buffer.shape
    half = count // 2

    def fetch(i):
        for core, pair in enumerate(((own_ref, other_ref), (other_ref, own_ref))):

            @pl.when(core_ref[0] == core)
            def _(pair=pair):
                pltpu.make_async_copy(pair[i], weight_buffer.at[i], weight_sems.at[i]).start()

    arriving, at = [[], []], 0
    for s, ref in enumerate(row_refs):
        if s == 0:
            fetch(1)
        elif s == len(row_refs) // 2:
            fetch(0)
        piece = row_buffer.at[at // rows, pl.ds(at % rows, ref.shape[0])]
        copy = pltpu.make_async_copy(ref, piece, row_sems.at[s])
        copy.start()
        arriving[at // (half * rows)].append(copy)
        at += ref.shape[0]
    leaving = []
    for i, buffer, out_ref in ((1, away_buffer, away_ref), (0, mine_buffer, mine_ref)):
        pltpu.make_async_copy(own_ref, weight_buffer.at[i], weight_sems.at[i]).wait()
        for h in range(2):
            if i == 1:
                for copy in arriving[h]:
                    copy.wait()
            product = jnp.dot(
                row_buffer[h * half : (h + 1) * half].reshape(half * rows, depth),
                weight_buffer[i],
                preferred_element_type=jnp.float32,
            ).astype(jnp.bfloat16)
            for s in range(half):
                k = h * half + s
                buffer[k] = product[s * rows : (s + 1) * rows]
                copy = pltpu.make_async_copy(
                    buffer.at[k], out_ref.at[places_ref[k]], out_sems.at[i * count + k]
                )
                copy.start()
                leaving.append(copy)
    for copy in leaving:
        copy.wait()


def project(core, places, gathered, own, other):
    rows, depth = gathered[0].shape
    count = sum(part.shape[0] for part in gathered) // rows
    columns = own.shape[1]
    scalars = pl.BlockSpec(memory_space=pltpu.SMEM)
    far = pl.BlockSpec(memory_space=pl.ANY)
    return pl.pallas_call(
        project_kernel,
        in_specs=[scalars, scalars] + [far] * (len(gathered) + 2),
        out_specs=[far, far],
        out_shape=[jax.ShapeDtypeStruct((count, rows, columns), jnp.bfloat16)] * 2,
        scratch_shapes=[
            pltpu.VMEM((count, rows, depth), jnp.bfloat16),
            pltpu.VMEM((2, depth, columns), jnp.bfloat16),
            pltpu.VMEM((count, rows, columns), jnp.bfloat16),
            pltpu.VMEM((count, rows, columns), jnp.bfloat16),
            pltpu.SemaphoreType.DMA((len(gathered),)),
            pltpu.SemaphoreType.DMA((2,)),
            pltpu.SemaphoreType.DMA((2 * count,)),
        ],
        compiler_params=pltpu.CompilerParams(vmem_limit_bytes=56 * 1024 * 1024),
        cost_estimate=pl.CostEstimate(
            flops=4 * count * rows * depth * columns,
            bytes_accessed=2 * (count * rows * (depth + 2 * columns) + 2 * depth * columns),
            transcendentals=0,
        ),
    )(core.reshape(1), places, *gathered, own, other)


def add_kernel(a_ref, b_ref, out_ref):
    total = a_ref[...].astype(jnp.float32) + b_ref[...].astype(jnp.float32)
    out_ref[...] = total.astype(jnp.bfloat16)


def add(a, b):
    count, rows, columns = a.shape
    block = pl.BlockSpec((2, rows, columns), lambda i: (i, 0, 0))
    return pl.pallas_call(
        add_kernel,
        grid=(count // 2,),
        in_specs=[block, block],
        out_specs=block,
        out_shape=jax.ShapeDtypeStruct(a.shape, jnp.bfloat16),
        compiler_params=pltpu.CompilerParams(vmem_limit_bytes=24 * 1024 * 1024),
        cost_estimate=pl.CostEstimate(
            flops=count * rows * columns, bytes_accessed=6 * count * rows * columns, transcendentals=0
        ),
    )(a, b)


def output_kernel(core_ref, rows_ref, weight_ref, *refs):
    out_ref = refs[-1]
    xs, _, rows, _ = out_ref.shape
    product = jnp.dot(
        rows_ref[...], weight_ref[...], preferred_element_type=jnp.float32
    ).astype(jnp.bfloat16)
    for x in range(xs):
        out_ref[x, 0] = product[x * rows : (x + 1) * rows]


def output(core, value, weight, xs, buffer=None):
    rows, depth = value.shape
    columns = weight.shape[1]
    step = 256
    shape = (xs, 2, rows // xs, columns)
    grid_spec = pltpu.PrefetchScalarGridSpec(
        num_scalar_prefetch=1,
        grid=(columns // step,),
        in_specs=[
            pl.BlockSpec((rows, depth), lambda n, core: (0, 0)),
            pl.BlockSpec((depth, step), lambda n, core: (0, n)),
        ]
        + ([] if buffer is None else [pl.BlockSpec(memory_space=pl.ANY)]),
        out_specs=pl.BlockSpec((xs, 1, rows // xs, step), lambda n, core: (0, core[0], 0, n)),
    )
    return pl.pallas_call(
        output_kernel,
        grid_spec=grid_spec,
        out_shape=jax.ShapeDtypeStruct(shape, jnp.bfloat16),
        input_output_aliases={} if buffer is None else {3: 0},
        compiler_params=pltpu.CompilerParams(vmem_limit_bytes=32 * 1024 * 1024),
        cost_estimate=pl.CostEstimate(
            flops=2 * rows * depth * columns,
            bytes_accessed=2 * (rows * (depth + columns) + depth * columns),
            transcendentals=0,
        ),
    )(core.reshape(1), value, weight, *([] if buffer is None else [buffer]))


SWAP = [(0, 1), (1, 0)]


def shifted(value, axis, shift):
    size = lax.axis_size(axis)
    return lax.ppermute(value, axis, [(i, (i + shift) % size) for i in range(size)])


def beside(value, axis):
    return [value, shifted(value, axis, 1), shifted(value, axis, 3)]


def relayed(blocks, axis):
    value, near, back = blocks
    half = value.shape[0] // 2
    return [value, near, shifted(near[:half], axis, 1), shifted(back[half:], axis, 3), back]


def body(normed, qkv_weight, out_weight, prompt_key_value, beam_key_value, parents, lengths):
    prompts = prompt_key_value.shape[0]
    beams = BEAMS_PER_PROMPT
    nx, nz, ny = lax.axis_size("x"), lax.axis_size("z"), lax.axis_size("y")
    core = lax.axis_index("core")
    z, y = lax.axis_index("z"), lax.axis_index("y")
    depth, columns = qkv_weight.shape
    mine_rows = prompts * beams

    other = lax.ppermute(qkv_weight, "y", [(i, ny - 1 - i) for i in range(ny)])
    own = beside(normed, "z")
    swapped = lax.ppermute(normed, "y", [(i, i ^ 1) for i in range(ny)])
    tables = rotary_tables(lengths + beam_key_value.shape[1])
    slab = jnp.arange(nz * ny, dtype=jnp.int32)
    slab_z, slab_y = slab // ny, slab % ny
    slots = jnp.where(slab_y // 2 == core, 0, 1)
    sender_y = jnp.where(slots == 0, slab_y, ny - 1 - slab_y)
    sources = (jnp.where(slots == core, 0, nz) + slab_z) * 2 + sender_y % 2
    sources = sources.astype(jnp.int32)
    from_z = (z - jnp.arange(nz, dtype=jnp.int32)) % nz
    places = jnp.concatenate([from_z * 2 + y % 2, from_z * 2 + 1 - y % 2]).astype(jnp.int32)
    core = core.astype(jnp.int32)
    small = (tables, sources, places)
    (*own, swapped), small = lax.optimization_barrier(((*own, swapped), small))
    tables, sources, places = small
    swapped = beside(swapped, "z")
    own = relayed(own, "z")
    swapped = relayed(swapped, "z")
    out_weight, other = lax.optimization_barrier((out_weight, other))
    weight = lax.all_gather(out_weight, "y", axis=0, tiled=True)

    history = beam_key_value.reshape(-1, beam_key_value.shape[-1])
    mine, away = project(core, places, own + swapped, qkv_weight, other)
    terms = add(mine, lax.ppermute(away, "core", SWAP))
    terms = terms.reshape(nx * nz * ny, mine_rows, columns)
    terms = lax.all_to_all(terms, ("x", "z", "y"), split_axis=0, concat_axis=0, tiled=True)
    terms = jnp.sum(terms.reshape(nx, nz, 2, 2, mine_rows, columns).astype(jnp.float32), axis=0)
    terms = terms.astype(jnp.bfloat16)
    kept = lax.dynamic_index_in_dim(terms, core, 1, keepdims=False)
    passed = lax.dynamic_index_in_dim(terms, 1 - core, 1, keepdims=False)
    terms = jnp.stack([kept, lax.ppermute(passed, "core", SWAP)])
    terms = terms.reshape(4 * nz, prompts, beams, columns)
    out, fresh = attend(
        terms, sources, tables, prompt_key_value, history, parents, lengths, nz, nx
    )
    copies = out.reshape(nx * nz, mine_rows, -1)
    mine = lax.all_to_all(copies, ("x", "z"), split_axis=0, concat_axis=0, tiled=True)
    mine = mine.reshape(nx * nz * mine_rows, -1)
    twin = lax.ppermute(mine, "core", SWAP)
    product = output(core, mine, weight, nx)
    product = output(1 - core, twin, weight, nx, product)
    product = product.reshape(nz * ny, 2 * mine_rows, -1)
    terms = lax.all_to_all(product, ("z", "y"), split_axis=0, concat_axis=0, tiled=True)
    terms = terms.reshape(nz, ny, 2, mine_rows, -1).astype(jnp.float32)
    result = jnp.sum(terms, axis=0).astype(jnp.bfloat16).transpose(1, 0, 2, 3)
    return (result.reshape(-1, result.shape[-1]), fresh.reshape(mine_rows, -1))


def solution(mesh):
    chips = Mesh(mesh.devices.reshape(4, 2, 4, 4), ("x", "core", "z", "y"))
    gx, gy = ("x", "core"), ("z", "y")
    whole = gx + gy
    return jax.shard_map(
        body,
        mesh=chips,
        in_specs=(
            P(gy, gx),
            P(gx, gy),
            P(gy, gx),
            P(whole, None, None),
            P(whole, None, None),
            P(whole),
            P(whole),
        ),
        out_specs=(P(gy, gx), P(whole, None)),
        check_vma=False,
    )
```
